128 devices in a mesh: node: 16 (over x_hi, y, core), local: 8 (over z, x_lo).
Axes of the slice: x: 4 (x_hi: 2, x_lo: 2; x = x_hi * 2 + x_lo), y: 4, z: 4, core: 2. Of those that a mesh axis runs over, the one named last changes fastest.
Arguments:
- output_grad: bfloat16 [65536, 768], P(('node', 'local')), may hold values from -6 to 6
- gate_prob: float32 [65536], P(('node', 'local')), may hold values from 0.2 to 1
- expert_ids: int32 [65536], P(('node', 'local')), may hold values from 0 to 127, as said below
- slots: int32 [65536], P(('node', 'local')), may hold values from -1 to 4, as said below
- expert_inputs: bfloat16 [128, 640, 768], P(('node', 'local')), may hold values from -6 to 6
- w_in: bfloat16 [128, 768, 3072], P(('node', 'local')), may hold values from -0.21875 to 0.21875
- w_out: bfloat16 [128, 3072, 768], P(('node', 'local')), may hold values from -0.109375 to 0.109375
Outputs:
- token_grad: bfloat16 [65536, 768], P(('node', 'local'))
- gate_grad: float32 [65536], P(('node', 'local'))
- w_in_grad: bfloat16 [128, 768, 3072], P(('node', 'local'))
- w_out_grad: bfloat16 [128, 3072, 768], P(('node', 'local'))
The draws below stay inside these ranges and needn't reach their ends.
Inputs may be any that keep to these rules, and one draw needn't show every extreme that they name: `expert_ids`: on every device some expert (the same on all devices) is chosen by more than 5 of its tokens. slots[t] counts the earlier tokens of the same device with the same expert; tokens with count 5 or more are dropped and have -1. On every device some token takes slot 4, the last of its expert's 5 slots.
All inputs are finite; a program needn't handle non-finite values.
Results may differ from the reference program's by a relative error of at most 0.0058.
Values may be sent and summed in bfloat16 or wider, within the bound.
A program may use at most 128 MiB of HBM per device.

```python
import math
import jax
import jax.numpy as jnp
from jax import lax

D = 768
FF = 3072
TOK_DEV = 512
EXPERTS = 128
TOKENS = 65536
CAP = 5
ROWS = 640


def draw_routing(key):
    blocks = TOKENS // TOK_DEV
    key_ids, key_plant, key_start = jax.random.split(jax.random.fold_in(key, 11), 3)
    chosen = jax.random.randint(key_ids, (blocks, TOK_DEV), 0, EXPERTS)
    planted = jax.random.randint(key_plant, (), 0, EXPERTS)
    start = jax.random.randint(key_start, (blocks, 1), 0, TOK_DEV)
    position = jnp.arange(TOK_DEV, dtype=jnp.int32)[None, :]
    inside = (position - start) % TOK_DEV < CAP + 2
    chosen = jnp.where(inside, planted, chosen).astype(jnp.int32)
    onehot = (chosen[:, :, None] == jnp.arange(EXPERTS, dtype=jnp.int32)[None, None, :]).astype(jnp.int32)
    running = jnp.cumsum(onehot, axis=1)
    rank = jnp.sum(onehot * running, axis=2) - 1
    slot_of = jnp.where(rank < CAP, rank, -1).astype(jnp.int32)
    return (chosen.reshape(TOKENS), slot_of.reshape(TOKENS))


def draw_expert_ids(key, part):
    chosen, slot_of = draw_routing(key)
    return chosen


def draw_slots(key, part):
    chosen, slot_of = draw_routing(key)
    return slot_of


def levels(rng, dims, shards, low, high):
    loudness = 1.0
    for dim, parts in shards:
        heights = jax.random.uniform(jax.random.fold_in(jax.random.fold_in(rng, 6), dim), (parts,), jnp.float32, low / len(shards), high / len(shards))
        loudness = loudness * jnp.repeat(jnp.exp(heights), dims[dim] // parts).reshape((-1,) + (1,) * (len(dims) - 1 - dim))
    return loudness


def normal_values(stream_key, shape, scale, limit, pieces=(), kind=jnp.bfloat16):
    entries = jax.random.normal(stream_key, shape, jnp.float32) * scale
    if len(pieces) > 0:
        entries = levels(stream_key, shape, pieces, -0.22, 0.18) * entries
    return jnp.clip(entries, min=-limit, max=limit).astype(kind)


def setup_inputs(seed: int = 0) -> dict:
    streams_of = jax.random.split(jax.random.key(seed), 8)
    output_grad = normal_values(streams_of[0], (TOKENS, D), 1.0, 6.0, ((0, 128),))
    gate_prob = jnp.clip(0.2 + 0.8 * jax.random.uniform(streams_of[1], (TOKENS,), jnp.float32) ** levels(streams_of[1], (TOKENS,), ((0, 128),), -0.2, 0.2), 0.2, 1.0)
    expert_ids = draw_expert_ids(jax.random.fold_in(streams_of[7], 71), 0)
    slots = draw_slots(jax.random.fold_in(streams_of[7], 71), 0)
    expert_inputs = normal_values(streams_of[4], (EXPERTS, ROWS, D), 1.0, 6.0, ((0, 128),))
    w_in = normal_values(streams_of[5], (EXPERTS, D, FF), D ** -0.5, 0.21875, ((0, 128),))
    w_out = normal_values(streams_of[6], (EXPERTS, FF, D), FF ** -0.5, 0.109375, ((0, 128),))
    return {"output_grad": output_grad, "gate_prob": gate_prob, "expert_ids": expert_ids, "slots": slots, "expert_inputs": expert_inputs, "w_in": w_in, "w_out": w_out}


def normal_parts(pre):
    cdf = 0.5 * (1.0 + jax.scipy.special.erf(pre / math.sqrt(2.0)))
    dens = jnp.exp(-0.5 * pre * pre) / math.sqrt(2.0 * math.pi)
    return (cdf, dens)

def expert_backward(items):
    routed_rows, inputs, weight_in, weight_out = items
    pre = jnp.dot(inputs, weight_in, preferred_element_type=jnp.float32)
    cdf, dens = normal_parts(pre)
    hidden = (pre * cdf).astype(jnp.bfloat16)
    expert_out = jnp.dot(hidden, weight_out, preferred_element_type=jnp.float32).astype(jnp.bfloat16)
    hidden_grad = lax.dot_general(routed_rows, weight_out, (((1,), (1,)), ((), ())), preferred_element_type=jnp.float32)
    pre_grad = (hidden_grad * (cdf + pre * dens)).astype(jnp.bfloat16)
    input_grad = lax.dot_general(pre_grad, weight_in, (((1,), (1,)), ((), ())), preferred_element_type=jnp.float32).astype(jnp.bfloat16)
    out_grad = lax.dot_general(hidden, routed_rows, (((0,), (0,)), ((), ())), preferred_element_type=jnp.float32).astype(jnp.bfloat16)
    in_grad = lax.dot_general(inputs, pre_grad, (((0,), (0,)), ((), ())), preferred_element_type=jnp.float32).astype(jnp.bfloat16)
    return (input_grad, expert_out, in_grad, out_grad)

def reference(output_grad, gate_prob, expert_ids, slots, expert_inputs, w_in, w_out):
    rows = expert_inputs.shape[1]
    scaled = (gate_prob[:, None] * output_grad.astype(jnp.float32)).astype(jnp.bfloat16)
    source = (jnp.arange(TOKENS, dtype=jnp.int32) // TOK_DEV).astype(jnp.int32)
    keep = slots >= 0
    target = jnp.where(keep, expert_ids * rows + source * CAP + slots, EXPERTS * rows).astype(jnp.int32)
    routed = jnp.zeros((EXPERTS * rows, D), jnp.bfloat16).at[target].set(scaled, mode='drop')
    routed = routed.reshape(EXPERTS, rows, D)
    input_grad, expert_out, in_grad, out_grad = lax.map(expert_backward, (routed, expert_inputs, w_in, w_out))
    picked = jnp.minimum(target, EXPERTS * rows - 1).astype(jnp.int32)
    back_grad = input_grad.reshape(EXPERTS * rows, D)[picked]
    back_out = expert_out.reshape(EXPERTS * rows, D)[picked]
    token_grad = jnp.where(keep[:, None], back_grad, jnp.zeros_like(back_grad))
    product = lax.optimization_barrier(jnp.sum(output_grad.astype(jnp.float32) * back_out.astype(jnp.float32), axis=1))
    gate_grad = jnp.where(keep, product, jnp.float32(0.0))
    return (token_grad, gate_grad, in_grad, out_grad)
```

```python
import functools
import math

import jax
import jax.numpy as jnp
from jax import lax
from jax.experimental import pallas as pl
from jax.experimental.pallas import tpu as pltpu
from jax.sharding import PartitionSpec as P

MESH = pl.DeviceIdType.MESH
F32 = jnp.float32
BF16 = jnp.bfloat16
LANES = 128
MSG = 32
NT = (((1,), (1,)), ((), ()))
TN = (((0,), (0,)), ((), ()))
VMEM_LIMIT = 60 * 1024 * 1024


def signal(sem, device):
    pl.semaphore_signal(sem, inc=1, device_id=device, device_id_type=MESH)


def exchange_kernel(
    n_node, n_local, cap, ids, slots, gate, og_hbm, x_hbm, win_hbm, wout_hbm,
    back, hid_t_hbm, pg_hbm, x_t_hbm, routed_hbm,
    og, x, win, wout, xp, x_t, hid, hid_t, slope, pg, routed, wide, msg, recv, ret,
    in_sem, out_sem, own_sem, send_sem, recv_sem, back_send_sem, back_recv_sem,
):
    node, local = lax.axis_index("node"), lax.axis_index("local")
    n_dev = n_node * n_local
    me = node * n_local + local
    core, pair = node % 2, node // 2
    n_pair = n_node // 2
    part = n_pair * n_local
    place = pair * n_local + local
    rows, width = xp.shape
    half = part * cap
    blocks = width // LANES
    ff = hid.shape[1]

    loads = [
        pltpu.make_async_copy(src, dst, in_sem.at[k])
        for k, (src, dst) in enumerate(((og_hbm, og), (x_hbm, x), (win_hbm, win), (wout_hbm, wout)))
    ]
    for load in loads:
        load.start()

    barrier = pltpu.get_barrier_semaphore()

    def greet(k, carry):
        for j in range(n_local):
            signal(barrier, ((node + k) % n_node, j))
        return carry

    lax.fori_loop(1, n_node, greet, 0)
    for j in range(1, n_local):
        signal(barrier, (node, (local + j) % n_local))

    loads[0].wait()
    target = jnp.where(slots[...] >= 0, slots[...] * n_dev + ids[...], -1)
    tokens = target.shape[1]
    for c in range(cap):
        hit = lax.broadcasted_iota(jnp.int32, (n_dev, tokens), 0) + c * n_dev == target
        moved = jnp.dot(hit.astype(BF16), og[...], preferred_element_type=F32)
        factor = jnp.sum(jnp.where(hit, gate[...], 0.0), axis=1, keepdims=True)
        moved = moved * factor
        for b in range(blocks):
            wide[pl.ds(c * blocks + b, n_dev, stride=MSG), :] = moved[:, b * LANES : (b + 1) * LANES]
    msg[...] = wide[...].reshape(n_dev, MSG, LANES).astype(BF16)

    pl.semaphore_wait(barrier, n_dev - 1)

    def peer(step, k):
        there = (place + k) % part
        return 2 * (there // n_local) + (core + step) % 2, there % n_local, there

    own = pltpu.make_async_copy(msg.at[me], recv.at[0, place], own_sem)
    own.start()
    for step in range(2):

        def send(k, carry, step=step):
            to_node, to_local, there = peer(step, k)
            pltpu.make_async_remote_copy(
                src_ref=msg.at[to_node * n_local + to_local],
                dst_ref=recv.at[step, place],
                send_sem=send_sem,
                recv_sem=recv_sem.at[step],
                device_id=(to_node, to_local),
                device_id_type=MESH,
            ).start()
            return carry

        lax.fori_loop(1 - step, part, send, 0)

    loads[1].wait()
    for step in range(2):
        r = lax.broadcasted_iota(jnp.int32, (half, rows), 0)
        c, i = r // part, r % part
        source = (i // n_local) * (2 * n_local) + ((core + step) % 2) * n_local + i % n_local
        hit = lax.broadcasted_iota(jnp.int32, (half, rows), 1) == source * cap + c
        ordered = jnp.dot(hit.astype(BF16), x[...], preferred_element_type=F32).astype(BF16)
        xp[step * half : (step + 1) * half, :] = ordered

    loads[2].wait()
    tile = 256

    def forward(k, carry):
        cols = pl.ds(pl.multiple_of(k * tile, tile), tile)
        pre = jnp.dot(xp[...], win[:, cols], preferred_element_type=F32)
        cdf = 0.5 * (1.0 + lax.erf(pre * (1.0 / math.sqrt(2.0))))
        dens = jnp.exp(-0.5 * pre * pre) * (1.0 / math.sqrt(2.0 * math.pi))
        hidden = (pre * cdf).astype(BF16)
        hid[:, cols] = hidden
        hid_t[cols, :] = hidden.T
        slope[:, cols] = cdf + pre * dens
        return carry

    lax.fori_loop(0, ff // tile, forward, 0)
    x_t[...] = xp[...].T
    stores = [
        pltpu.make_async_copy(src, dst, out_sem.at[k])
        for k, (src, dst) in enumerate(
            ((hid_t, hid_t_hbm), (x_t, x_t_hbm), (pg, pg_hbm), (routed, routed_hbm))
        )
    ]
    stores[0].start()
    stores[1].start()
    own.wait()
    loads[3].wait()

    own_back = pltpu.make_async_copy(ret.at[0, place], back.at[me], own_sem)
    for step in range(2):
        mine = slice(step * half, (step + 1) * half)
        n_in = part - 1 + step
        got = recv.at[step, pl.ds(0, n_in)]
        pltpu.make_async_copy(got, got, recv_sem.at[step]).wait()
        wide[0 : part * MSG, :] = recv[step].astype(F32).reshape(part * MSG, LANES)
        for c in range(cap):
            for b in range(blocks):
                routed[step * half + c * part : step * half + (c + 1) * part, b * LANES : (b + 1) * LANES] = (
                    wide[pl.ds(c * blocks + b, part, stride=MSG), :].astype(BF16)
                )

        def backward(k, total, mine=mine):
            cols = pl.ds(pl.multiple_of(k * tile, tile), tile)
            up = lax.dot_general(routed[mine, :], wout[cols, :], NT, preferred_element_type=F32)
            pg[mine, cols] = (up * slope[mine, cols]).astype(BF16)
            both = up * hid[mine, cols].astype(F32)
            for b in range(tile // LANES):
                total = total + both[:, b * LANES : (b + 1) * LANES]
            return total

        total = lax.fori_loop(0, ff // tile, backward, jnp.zeros((half, LANES), F32))
        product = jnp.sum(total, axis=1, keepdims=True)
        lane = lax.broadcasted_iota(jnp.int32, (part, LANES), 1)
        spread = jnp.zeros((part, LANES), F32)
        for c in range(cap):
            spread = jnp.where(lane == c, product[c * part : (c + 1) * part], spread)
        high = spread.astype(BF16).astype(F32)
        wide[pl.ds(cap * blocks, part, stride=MSG), :] = high
        wide[pl.ds(cap * blocks + 1, part, stride=MSG), :] = spread - high
        for q in range(width // 256):
            down = lax.dot_general(
                pg[mine, :], win[q * 256 : (q + 1) * 256, :], NT, preferred_element_type=F32
            )
            for c in range(cap):
                for b in range(2):
                    wide[pl.ds(c * blocks + 2 * q + b, part, stride=MSG), :] = down[
                        c * part : (c + 1) * part, b * LANES : (b + 1) * LANES
                    ]
        ret[step] = wide[0 : part * MSG, :].reshape(part, MSG, LANES).astype(BF16)
        if step == 0:
            own_back.start()

        def reply(k, carry, step=step):
            to_node, to_local, there = peer(step, k)
            pltpu.make_async_remote_copy(
                src_ref=ret.at[step, there],
                dst_ref=back.at[me],
                send_sem=back_send_sem,
                recv_sem=back_recv_sem,
                device_id=(to_node, to_local),
                device_id_type=MESH,
            ).start()
            return carry

        lax.fori_loop(1 - step, part, reply, 0)

    stores[2].start()
    stores[3].start()
    sent = msg.at[pl.ds(0, n_dev - 1)]
    pltpu.make_async_copy(sent, sent, send_sem).wait()
    pltpu.make_async_copy(sent, sent, back_send_sem).wait()
    came = back.at[pl.ds(0, n_dev - 1)]
    own_back.wait()
    for store in stores:
        store.wait()
    pltpu.make_async_copy(came, came, back_recv_sem).wait()


def weights_kernel(
    cap, ids, slots, gate, back, hid_t, pg, x_t, routed, token_grad, gate_grad, in_grad, out_grad, wide, rows_back
):
    out_grad[...] = jnp.dot(hid_t[...], routed[...], preferred_element_type=F32).astype(BF16)
    in_grad[...] = jnp.dot(x_t[...], pg[...], preferred_element_type=F32).astype(BF16)

    @pl.when(pl.program_id(0) == 0)
    def _():
        n_dev = back.shape[0]
        tokens, width = token_grad.shape
        blocks = width // LANES
        wide[...] = back[...].astype(F32).reshape(n_dev * MSG, LANES)
        for c in range(cap):
            for b in range(blocks):
                rows_back[c * n_dev : (c + 1) * n_dev, b * LANES : (b + 1) * LANES] = wide[
                    pl.ds(c * blocks + b, n_dev, stride=MSG), :
                ].astype(BF16)
        high = wide[pl.ds(cap * blocks, n_dev, stride=MSG), :].astype(BF16)
        low = wide[pl.ds(cap * blocks + 1, n_dev, stride=MSG), :].astype(BF16)
        target = jnp.where(slots[...] >= 0, slots[...] * n_dev + ids[...], -1)
        column = jnp.broadcast_to(target.astype(F32), (LANES, tokens)).T
        lane = lax.broadcasted_iota(jnp.int32, (tokens, LANES), 1).astype(F32)
        hits = [
            jnp.where(column == lane + (k * LANES), 1.0, 0.0).astype(BF16)
            for k in range(cap * n_dev // LANES)
        ]
        token_grad[...] = jnp.dot(
            jnp.concatenate(hits, axis=1), rows_back[...], preferred_element_type=F32
        ).astype(BF16)
        expert = lax.broadcasted_iota(jnp.int32, (n_dev, tokens), 0) == ids[...]
        expert = expert.astype(BF16)
        products = lax.dot_general(high, expert, TN, preferred_element_type=F32)
        products += lax.dot_general(low, expert, TN, preferred_element_type=F32)
        chosen = lax.broadcasted_iota(jnp.int32, (LANES, tokens), 0) == slots[...]
        picked = jnp.sum(jnp.where(chosen, products, 0.0)[0:8], axis=0, keepdims=True)
        gate_grad[...] = picked / gate[...]


def shards(output_grad, gate_prob, expert_ids, slots, expert_inputs, w_in, w_out):
    n_node = lax.axis_size("node")
    n_local = lax.axis_size("local")
    n_dev = n_node * n_local
    rows = expert_inputs.shape[1]
    cap = rows // n_dev
    tokens, width = output_grad.shape
    ff = w_in.shape[2]
    ids = expert_ids.reshape(1, tokens)
    place = slots.reshape(1, tokens)
    gate = gate_prob.reshape(1, tokens)
    anywhere = pl.BlockSpec(memory_space=pl.ANY)
    vmem = pl.BlockSpec(memory_space=pltpu.VMEM)
    part = n_dev // 2
    dma = pltpu.SemaphoreType.DMA
    back, hid_t, pg, x_t, routed = pl.pallas_call(
        functools.partial(exchange_kernel, n_node, n_local, cap),
        out_shape=[
            jax.ShapeDtypeStruct((n_dev, MSG, LANES), BF16),
            jax.ShapeDtypeStruct((ff, rows), BF16),
            jax.ShapeDtypeStruct((rows, ff), BF16),
            jax.ShapeDtypeStruct((width, rows), BF16),
            jax.ShapeDtypeStruct((rows, width), BF16),
        ],
        in_specs=[vmem] * 3 + [anywhere] * 4,
        out_specs=[anywhere] * 5,
        scratch_shapes=[
            pltpu.VMEM((tokens, width), BF16),
            pltpu.VMEM((rows, width), BF16),
            pltpu.VMEM((width, ff), BF16),
            pltpu.VMEM((ff, width), BF16),
            pltpu.VMEM((rows, width), BF16),
            pltpu.VMEM((width, rows), BF16),
            pltpu.VMEM((rows, ff), BF16),
            pltpu.VMEM((ff, rows), BF16),
            pltpu.VMEM((rows, ff), F32),
            pltpu.VMEM((rows, ff), BF16),
            pltpu.VMEM((rows, width), BF16),
            pltpu.VMEM((n_dev * MSG, LANES), F32),
            pltpu.VMEM((n_dev, MSG, LANES), BF16),
            pltpu.VMEM((2, part, MSG, LANES), BF16),
            pltpu.VMEM((2, part, MSG, LANES), BF16),
            dma((4,)),
            dma((4,)),
            dma,
            dma,
            dma((2,)),
            dma,
            dma,
        ],
        compiler_params=pltpu.CompilerParams(
            collective_id=0, has_side_effects=True, vmem_limit_bytes=VMEM_LIMIT
        ),
        name="exchange",
    )(ids, place, gate, output_grad, expert_inputs[0], w_in[0], w_out[0])

    tile = 512
    whole = lambda *shape: pl.BlockSpec(shape, lambda k: (0,) * len(shape))
    token_grad, gate_grad, in_grad, out_grad = pl.pallas_call(
        functools.partial(weights_kernel, cap),
        grid=(ff // tile,),
        out_shape=[
            jax.ShapeDtypeStruct((tokens, width), BF16),
            jax.ShapeDtypeStruct((1, tokens), F32),
            jax.ShapeDtypeStruct((width, ff), BF16),
            jax.ShapeDtypeStruct((ff, width), BF16),
        ],
        in_specs=[
            whole(1, tokens),
            whole(1, tokens),
            whole(1, tokens),
            whole(n_dev, MSG, LANES),
            pl.BlockSpec((tile, rows), lambda k: (k, 0)),
            pl.BlockSpec((rows, tile), lambda k: (0, k)),
            whole(width, rows),
            whole(rows, width),
        ],
        out_specs=[
            whole(tokens, width),
            whole(1, tokens),
            pl.BlockSpec((width, tile), lambda k: (0, k)),
            pl.BlockSpec((tile, width), lambda k: (k, 0)),
        ],
        scratch_shapes=[pltpu.VMEM((n_dev * MSG, LANES), F32), pltpu.VMEM((rows, width), BF16)],
        compiler_params=pltpu.CompilerParams(vmem_limit_bytes=VMEM_LIMIT),
        name="weights",
    )(ids, place, gate, back, hid_t, pg, x_t, routed)
    return (token_grad, gate_grad.reshape(tokens), in_grad[None], out_grad[None])


def solution(mesh):
    placed = (
        P(("node", "local"), None),
        P(("node", "local")),
        P(("node", "local")),
        P(("node", "local")),
        P(("node", "local"), None, None),
        P(("node", "local"), None, None),
        P(("node", "local"), None, None),
    )
    return jax.shard_map(
        shards,
        mesh=mesh,
        in_specs=placed,
        out_specs=(
            P(("node", "local"), None),
            P(("node", "local")),
            P(("node", "local"), None, None),
            P(("node", "local"), None, None),
        ),
        check_vma=False,
    )
```

```python
import functools
import math

import jax
import jax.numpy as jnp
from jax import lax
from jax.experimental import pallas as pl
from jax.experimental.pallas import tpu as pltpu
from jax.sharding import PartitionSpec as P

MESH = pl.DeviceIdType.MESH
F32 = jnp.float32
BF16 = jnp.bfloat16
LANES = 128
MSG = 32
NT = (((1,), (1,)), ((), ()))
TN = (((0,), (0,)), ((), ()))
VMEM_LIMIT = 44 * 1024 * 1024
FWD_TILE = 512
BWD_TILE = 512
GRAD_TILE = 512


def signal(sem, device):
    pl.semaphore_signal(sem, inc=1, device_id=device, device_id_type=MESH)


def exchange_kernel(
    n_node, n_local, cap, ids, slots, gate, og_hbm, x_hbm, win_hbm, wout_hbm,
    back, in_grad, out_grad,
    og, x, win, wout, xp, x_t, hid, hid_t, slope, pg, routed, wide, msg, recv, ret,
    in_sem, own_sem, send_sem, recv_sem, back_send_sem, back_recv_sem,
):
    node, local = lax.axis_index("node"), lax.axis_index("local")
    n_dev = n_node * n_local
    me = node * n_local + local
    core, pair = node % 2, node // 2
    n_pair = n_node // 2
    part = n_pair * n_local
    place = pair * n_local + local
    rows, width = xp.shape
    half = part * cap
    blocks = width // LANES
    ff = hid.shape[1]

    loads = [
        pltpu.make_async_copy(src, dst, in_sem.at[k])
        for k, (src, dst) in enumerate(((og_hbm, og), (x_hbm, x), (win_hbm, win), (wout_hbm, wout)))
    ]
    for load in loads:
        load.start()

    barrier = pltpu.get_barrier_semaphore()

    def greet(k, carry):
        for j in range(n_local):
            signal(barrier, ((node + k) % n_node, j))
        return carry

    lax.fori_loop(1, n_node, greet, 0)
    for j in range(1, n_local):
        signal(barrier, (node, (local + j) % n_local))

    loads[0].wait()
    target = jnp.where(slots[...] >= 0, slots[...] * n_dev + ids[...], -1)
    tokens = target.shape[1]
    for c in range(cap):
        hit = lax.broadcasted_iota(jnp.int32, (n_dev, tokens), 0) + c * n_dev == target
        moved = jnp.dot(hit.astype(BF16), og[...], preferred_element_type=F32)
        factor = jnp.sum(jnp.where(hit, gate[...], 0.0), axis=1, keepdims=True)
        moved = moved * factor
        for b in range(blocks):
            wide[pl.ds(c * blocks + b, n_dev, stride=MSG), :] = moved[:, b * LANES : (b + 1) * LANES]
    msg[...] = wide[...].reshape(n_dev, MSG, LANES).astype(BF16)

    pl.semaphore_wait(barrier, n_dev - 1)

    def peer(step, k):
        there = (place + k) % part
        return 2 * (there // n_local) + (core + step) % 2, there % n_local, there

    own = pltpu.make_async_copy(msg.at[me], recv.at[0, place], own_sem)
    own.start()
    for step in range(2):

        def send(k, carry, step=step):
            to_node, to_local, there = peer(step, k)
            pltpu.make_async_remote_copy(
                src_ref=msg.at[to_node * n_local + to_local],
                dst_ref=recv.at[step, place],
                send_sem=send_sem,
                recv_sem=recv_sem.at[step],
                device_id=(to_node, to_local),
                device_id_type=MESH,
            ).start()
            return carry

        lax.fori_loop(1 - step, part, send, 0)

    loads[1].wait()
    for step in range(2):
        r = lax.broadcasted_iota(jnp.int32, (half, rows), 0)
        c, i = r // part, r % part
        source = (i // n_local) * (2 * n_local) + ((core + step) % 2) * n_local + i % n_local
        hit = lax.broadcasted_iota(jnp.int32, (half, rows), 1) == source * cap + c
        ordered = jnp.dot(hit.astype(BF16), x[...], preferred_element_type=F32).astype(BF16)
        xp[step * half : (step + 1) * half, :] = ordered

    loads[2].wait()
    tile = FWD_TILE
    wide_tile = GRAD_TILE

    def forward(k, carry):
        cols = pl.ds(pl.multiple_of(k * tile, tile), tile)
        pre = jnp.dot(xp[...], win[:, cols], preferred_element_type=F32)
        cdf = 0.5 * (1.0 + lax.erf(pre * (1.0 / math.sqrt(2.0))))
        dens = jnp.exp(-0.5 * pre * pre) * (1.0 / math.sqrt(2.0 * math.pi))
        hidden = (pre * cdf).astype(BF16)
        hid[:, cols] = hidden
        hid_t[cols, :] = hidden.T
        slope[:, cols] = cdf + pre * dens
        return carry

    lax.fori_loop(0, ff // tile, forward, 0)
    x_t[...] = xp[...].T
    own.wait()
    loads[3].wait()
    tile = BWD_TILE

    own_back = pltpu.make_async_copy(ret.at[0, place], back.at[me], own_sem)
    for step in range(2):
        mine = slice(step * half, (step + 1) * half)
        n_in = part - 1 + step
        got = recv.at[step, pl.ds(0, n_in)]
        pltpu.make_async_copy(got, got, recv_sem.at[step]).wait()
        wide[0 : part * MSG, :] = recv[step].astype(F32).reshape(part * MSG, LANES)
        for c in range(cap):
            for b in range(blocks):
                routed[step * half + c * part : step * half + (c + 1) * part, b * LANES : (b + 1) * LANES] = (
                    wide[pl.ds(c * blocks + b, part, stride=MSG), :].astype(BF16)
                )

        def backward(k, total, mine=mine):
            cols = pl.ds(pl.multiple_of(k * tile, tile), tile)
            up = lax.dot_general(routed[mine, :], wout[cols, :], NT, preferred_element_type=F32)
            pg[mine, cols] = (up * slope[mine, cols]).astype(BF16)
            both = up * hid[mine, cols].astype(F32)
            for b in range(tile // LANES):
                total = total + both[:, b * LANES : (b + 1) * LANES]
            return total

        total = lax.fori_loop(0, ff // tile, backward, jnp.zeros((half, LANES), F32))
        product = jnp.sum(total, axis=1, keepdims=True)
        lane = lax.broadcasted_iota(jnp.int32, (part, LANES), 1)
        spread = jnp.zeros((part, LANES), F32)
        for c in range(cap):
            spread = jnp.where(lane == c, product[c * part : (c + 1) * part], spread)
        high = spread.astype(BF16).astype(F32)
        wide[pl.ds(cap * blocks, part, stride=MSG), :] = high
        wide[pl.ds(cap * blocks + 1, part, stride=MSG), :] = spread - high
        for q in range(width // 256):
            down = lax.dot_general(
                pg[mine, :], win[q * 256 : (q + 1) * 256, :], NT, preferred_element_type=F32
            )
            for c in range(cap):
                for b in range(2):
                    wide[pl.ds(c * blocks + 2 * q + b, part, stride=MSG), :] = down[
                        c * part : (c + 1) * part, b * LANES : (b + 1) * LANES
                    ]
        ret[step] = wide[0 : part * MSG, :].reshape(part, MSG, LANES).astype(BF16)
        if step == 0:
            own_back.start()

        def reply(k, carry, step=step):
            to_node, to_local, there = peer(step, k)
            pltpu.make_async_remote_copy(
                src_ref=ret.at[step, there],
                dst_ref=back.at[me],
                send_sem=back_send_sem,
                recv_sem=back_recv_sem,
                device_id=(to_node, to_local),
                device_id_type=MESH,
            ).start()
            return carry

        lax.fori_loop(1 - step, part, reply, 0)

    def out_tile(k, carry):
        part_rows = pl.ds(pl.multiple_of(k * wide_tile, wide_tile), wide_tile)
        out_grad[part_rows, :] = jnp.dot(
            hid_t[part_rows, :], routed[...], preferred_element_type=F32
        ).astype(BF16)
        return carry

    def in_tile(k, carry):
        cols = pl.ds(pl.multiple_of(k * wide_tile, wide_tile), wide_tile)
        in_grad[:, cols] = jnp.dot(x_t[...], pg[:, cols], preferred_element_type=F32).astype(BF16)
        return carry

    lax.fori_loop(0, ff // wide_tile, out_tile, 0)
    lax.fori_loop(0, ff // wide_tile, in_tile, 0)
    sent = msg.at[pl.ds(0, n_dev - 1)]
    pltpu.make_async_copy(sent, sent, send_sem).wait()
    pltpu.make_async_copy(sent, sent, back_send_sem).wait()
    came = back.at[pl.ds(0, n_dev - 1)]
    own_back.wait()
    pltpu.make_async_copy(came, came, back_recv_sem).wait()


def combine_kernel(
    cap, ids, slots, gate, back, in_vmem, out_vmem, token_grad, gate_grad, in_grad, out_grad, wide, rows_back, sem
):
    copies = [
        pltpu.make_async_copy(in_vmem, in_grad, sem.at[0]),
        pltpu.make_async_copy(out_vmem, out_grad, sem.at[1]),
    ]
    for copy in copies:
        copy.start()
    n_dev = back.shape[0]
    tokens, width = token_grad.shape
    blocks = width // LANES
    wide[...] = back[...].astype(F32).reshape(n_dev * MSG, LANES)
    for c in range(cap):
        for b in range(blocks):
            rows_back[c * n_dev : (c + 1) * n_dev, b * LANES : (b + 1) * LANES] = wide[
                pl.ds(c * blocks + b, n_dev, stride=MSG), :
            ].astype(BF16)
    high = wide[pl.ds(cap * blocks, n_dev, stride=MSG), :].astype(BF16)
    low = wide[pl.ds(cap * blocks + 1, n_dev, stride=MSG), :].astype(BF16)
    target = jnp.where(slots[...] >= 0, slots[...] * n_dev + ids[...], -1)
    column = jnp.broadcast_to(target.astype(F32), (LANES, tokens)).T
    lane = lax.broadcasted_iota(jnp.int32, (tokens, LANES), 1).astype(F32)
    hits = [
        jnp.where(column == lane + (k * LANES), 1.0, 0.0).astype(BF16)
        for k in range(cap * n_dev // LANES)
    ]
    token_grad[...] = jnp.dot(
        jnp.concatenate(hits, axis=1), rows_back[...], preferred_element_type=F32
    ).astype(BF16)
    expert = lax.broadcasted_iota(jnp.int32, (n_dev, tokens), 0) == ids[...]
    expert = expert.astype(BF16)
    products = lax.dot_general(high, expert, TN, preferred_element_type=F32)
    products += lax.dot_general(low, expert, TN, preferred_element_type=F32)
    chosen = lax.broadcasted_iota(jnp.int32, (LANES, tokens), 0) == slots[...]
    picked = jnp.sum(jnp.where(chosen, products, 0.0)[0:8], axis=0, keepdims=True)
    gate_grad[...] = picked / gate[...]
    for copy in copies:
        copy.wait()


def shards(output_grad, gate_prob, expert_ids, slots, expert_inputs, w_in, w_out):
    n_node = lax.axis_size("node")
    n_local = lax.axis_size("local")
    n_dev = n_node * n_local
    rows = expert_inputs.shape[1]
    cap = rows // n_dev
    tokens, width = output_grad.shape
    ff = w_in.shape[2]
    ids = expert_ids.reshape(1, tokens)
    place = slots.reshape(1, tokens)
    gate = gate_prob.reshape(1, tokens)
    anywhere = pl.BlockSpec(memory_space=pl.ANY)
    vmem = pl.BlockSpec(memory_space=pltpu.VMEM)
    part = n_dev // 2
    dma = pltpu.SemaphoreType.DMA
    back, in_vmem, out_vmem = pl.pallas_call(
        functools.partial(exchange_kernel, n_node, n_local, cap),
        out_shape=[
            pltpu.VMEM((n_dev, MSG, LANES), BF16),
            pltpu.VMEM((width, ff), BF16),
            pltpu.VMEM((ff, width), BF16),
        ],
        in_specs=[vmem] * 3 + [anywhere] * 4,
        out_specs=[vmem] * 3,
        scratch_shapes=[
            pltpu.VMEM((tokens, width), BF16),
            pltpu.VMEM((rows, width), BF16),
            pltpu.VMEM((width, ff), BF16),
            pltpu.VMEM((ff, width), BF16),
            pltpu.VMEM((rows, width), BF16),
            pltpu.VMEM((width, rows), BF16),
            pltpu.VMEM((rows, ff), BF16),
            pltpu.VMEM((ff, rows), BF16),
            pltpu.VMEM((rows, ff), F32),
            pltpu.VMEM((rows, ff), BF16),
            pltpu.VMEM((rows, width), BF16),
            pltpu.VMEM((n_dev * MSG, LANES), F32),
            pltpu.VMEM((n_dev, MSG, LANES), BF16),
            pltpu.VMEM((2, part, MSG, LANES), BF16),
            pltpu.VMEM((2, part, MSG, LANES), BF16),
            dma((4,)),
            dma,
            dma,
            dma((2,)),
            dma,
            dma,
        ],
        compiler_params=pltpu.CompilerParams(
            collective_id=0, has_side_effects=True, vmem_limit_bytes=VMEM_LIMIT
        ),
        name="exchange",
    )(ids, place, gate, output_grad, expert_inputs[0], w_in[0], w_out[0])

    token_grad, gate_grad, in_grad, out_grad = pl.pallas_call(
        functools.partial(combine_kernel, cap),
        out_shape=[
            jax.ShapeDtypeStruct((tokens, width), BF16),
            jax.ShapeDtypeStruct((1, tokens), F32),
            jax.ShapeDtypeStruct((width, ff), BF16),
            jax.ShapeDtypeStruct((ff, width), BF16),
        ],
        in_specs=[vmem] * 6,
        out_specs=[vmem, vmem, anywhere, anywhere],
        scratch_shapes=[
            pltpu.VMEM((n_dev * MSG, LANES), F32),
            pltpu.VMEM((rows, width), BF16),
            dma((2,)),
        ],
        compiler_params=pltpu.CompilerParams(vmem_limit_bytes=16 * 1024 * 1024),
        name="combine",
    )(ids, place, gate, back, in_vmem, out_vmem)
    return (token_grad, gate_grad.reshape(tokens), in_grad[None], out_grad[None])


def solution(mesh):
    placed = (
        P(("node", "local"), None),
        P(("node", "local")),
        P(("node", "local")),
        P(("node", "local")),
        P(("node", "local"), None, None),
        P(("node", "local"), None, None),
        P(("node", "local"), None, None),
    )
    return jax.shard_map(
        shards,
        mesh=mesh,
        in_specs=placed,
        out_specs=(
            P(("node", "local"), None),
            P(("node", "local")),
            P(("node", "local"), None, None),
            P(("node", "local"), None, None),
        ),
        check_vma=False,
    )
```

```python
import functools
import math

import jax
import jax.numpy as jnp
from jax import lax
from jax.experimental import pallas as pl
from jax.experimental.pallas import tpu as pltpu
from jax.sharding import PartitionSpec as P

MESH = pl.DeviceIdType.MESH
F32 = jnp.float32
BF16 = jnp.bfloat16
LANES = 128
MSG = 32
NT = (((1,), (1,)), ((), ()))
TN = (((0,), (0,)), ((), ()))
VMEM_LIMIT = 44 * 1024 * 1024
FWD_TILE = 1536
BWD_TILE = 3072
GRAD_TILE = 3072


def signal(sem, device):
    pl.semaphore_signal(sem, inc=1, device_id=device, device_id_type=MESH)


def exchange_kernel(
    n_node, n_local, cap, ids, slots, gate, og_hbm, x_hbm, win_hbm, wout_hbm,
    back, in_grad, out_grad,
    og, x, win, wout, xp, x_t, hid, slope, pg, routed, wide, msg, recv, ret,
    in_sem, own_sem, send_sem, recv_sem, back_send_sem, back_recv_sem,
):
    node, local = lax.axis_index("node"), lax.axis_index("local")
    n_dev = n_node * n_local
    me = node * n_local + local
    core, pair = node % 2, node // 2
    n_pair = n_node // 2
    part = n_pair * n_local
    place = pair * n_local + local
    rows, width = xp.shape
    half = part * cap
    blocks = width // LANES
    ff = hid.shape[1]

    loads = [
        pltpu.make_async_copy(src, dst, in_sem.at[k])
        for k, (src, dst) in enumerate(((og_hbm, og), (x_hbm, x), (win_hbm, win), (wout_hbm, wout)))
    ]
    for load in loads:
        load.start()

    barrier = pltpu.get_barrier_semaphore()

    def greet(k, carry):
        for j in range(n_local):
            signal(barrier, ((node + k) % n_node, j))
        return carry

    for k in range(1, n_node):
        greet(k, 0)
    for j in range(1, n_local):
        signal(barrier, (node, (local + j) % n_local))

    loads[0].wait()
    target = jnp.where(slots[...] >= 0, slots[...] * n_dev + ids[...], -1)
    tokens = target.shape[1]
    for c in range(cap):
        hit = lax.broadcasted_iota(jnp.int32, (n_dev, tokens), 0) + c * n_dev == target
        moved = jnp.dot(hit.astype(BF16), og[...], preferred_element_type=F32)
        factor = jnp.sum(jnp.where(hit, gate[...], 0.0), axis=1, keepdims=True)
        moved = moved * factor
        for b in range(blocks):
            wide[pl.ds(c * blocks + b, n_dev, stride=MSG), :] = moved[:, b * LANES : (b + 1) * LANES]
    msg[...] = wide[...].reshape(n_dev, MSG, LANES).astype(BF16)

    pl.semaphore_wait(barrier, n_dev - 1)

    def peer(step, k):
        there = (place + k) % part
        return 2 * (there // n_local) + (core + step) % 2, there % n_local, there

    own = pltpu.make_async_copy(msg.at[me], recv.at[0, place], own_sem)
    own.start()
    def send(step, k):
        to_node, to_local, there = peer(step, k)
        pltpu.make_async_remote_copy(
            src_ref=msg.at[to_node * n_local + to_local],
            dst_ref=recv.at[step, place],
            send_sem=send_sem,
            recv_sem=recv_sem.at[step],
            device_id=(to_node, to_local),
            device_id_type=MESH,
        ).start()

    for k in range(1, part):
        send(0, k)

    loads[1].wait()
    for step in range(2):
        r = lax.broadcasted_iota(jnp.int32, (half, rows), 0)
        c, i = r // part, r % part
        source = (i // n_local) * (2 * n_local) + ((core + step) % 2) * n_local + i % n_local
        hit = lax.broadcasted_iota(jnp.int32, (half, rows), 1) == source * cap + c
        ordered = jnp.dot(hit.astype(BF16), x[...], preferred_element_type=F32).astype(BF16)
        xp[step * half : (step + 1) * half, :] = ordered

    loads[2].wait()
    tile = FWD_TILE
    wide_tile = GRAD_TILE

    def forward(k, carry):
        cols = pl.ds(k * tile if isinstance(k, int) else pl.multiple_of(k * tile, tile), tile)
        pre = jnp.dot(xp[...], win[:, cols], preferred_element_type=F32)
        cdf = 0.5 * (1.0 + lax.erf(pre * (1.0 / math.sqrt(2.0))))
        dens = jnp.exp(-0.5 * pre * pre) * (1.0 / math.sqrt(2.0 * math.pi))
        hidden = (pre * cdf).astype(BF16)
        hid[:, cols] = hidden
        slope[:, cols] = cdf + pre * dens
        return carry

    n_tiles = ff // tile
    for t in range(n_tiles):
        forward(t, 0)
    for k in range(part):
        send(1, k)
    own.wait()
    loads[3].wait()
    tile = BWD_TILE

    own_back = pltpu.make_async_copy(ret.at[0, place], back.at[me], own_sem)
    for step in range(2):
        mine = slice(step * half, (step + 1) * half)
        n_in = part - 1 + step
        got = recv.at[step, pl.ds(0, n_in)]
        pltpu.make_async_copy(got, got, recv_sem.at[step]).wait()
        wide[0 : part * MSG, :] = recv[step].astype(F32).reshape(part * MSG, LANES)
        for c in range(cap):
            for b in range(blocks):
                routed[step * half + c * part : step * half + (c + 1) * part, b * LANES : (b + 1) * LANES] = (
                    wide[pl.ds(c * blocks + b, part, stride=MSG), :].astype(BF16)
                )

        def backward(k, total, mine=mine):
            cols = pl.ds(k * tile if isinstance(k, int) else pl.multiple_of(k * tile, tile), tile)
            up = lax.dot_general(routed[mine, :], wout[cols, :], NT, preferred_element_type=F32)
            pg[mine, cols] = (up * slope[mine, cols]).astype(BF16)
            both = up * hid[mine, cols].astype(F32)
            for b in range(tile // LANES):
                total = total + both[:, b * LANES : (b + 1) * LANES]
            return total

        total = lax.fori_loop(0, ff // tile, backward, jnp.zeros((half, LANES), F32))
        product = jnp.sum(total, axis=1, keepdims=True)
        lane = lax.broadcasted_iota(jnp.int32, (part, LANES), 1)
        spread = jnp.zeros((part, LANES), F32)
        for c in range(cap):
            spread = jnp.where(lane == c, product[c * part : (c + 1) * part], spread)
        high = spread.astype(BF16).astype(F32)
        wide[pl.ds(cap * blocks, part, stride=MSG), :] = high
        wide[pl.ds(cap * blocks + 1, part, stride=MSG), :] = spread - high
        for q in range(width // 256):
            down = lax.dot_general(
                pg[mine, :], win[q * 256 : (q + 1) * 256, :], NT, preferred_element_type=F32
            )
            for c in range(cap):
                for b in range(2):
                    wide[pl.ds(c * blocks + 2 * q + b, part, stride=MSG), :] = down[
                        c * part : (c + 1) * part, b * LANES : (b + 1) * LANES
                    ]
        ret[step] = wide[0 : part * MSG, :].reshape(part, MSG, LANES).astype(BF16)
        if step == 0:
            own_back.start()

        def reply(k, carry, step=step):
            to_node, to_local, there = peer(step, k)
            pltpu.make_async_remote_copy(
                src_ref=ret.at[step, there],
                dst_ref=back.at[me],
                send_sem=back_send_sem,
                recv_sem=back_recv_sem,
                device_id=(to_node, to_local),
                device_id_type=MESH,
            ).start()
            return carry

        for k in range(1 - step, part):
            reply(k, 0)

    def out_tile(k, carry):
        part_rows = pl.ds(pl.multiple_of(k * wide_tile, wide_tile), wide_tile)
        out_grad[part_rows, :] = lax.dot_general(
            hid[:, part_rows], routed[...], TN, preferred_element_type=F32
        ).astype(BF16)
        return carry

    x_t[...] = xp[...].T

    def in_tile(k, carry):
        cols = pl.ds(pl.multiple_of(k * wide_tile, wide_tile), wide_tile)
        in_grad[:, cols] = jnp.dot(x_t[...], pg[:, cols], preferred_element_type=F32).astype(BF16)
        return carry

    lax.fori_loop(0, ff // wide_tile, out_tile, 0)
    lax.fori_loop(0, ff // wide_tile, in_tile, 0)
    sent = msg.at[pl.ds(0, n_dev - 1)]
    pltpu.make_async_copy(sent, sent, send_sem).wait()
    pltpu.make_async_copy(sent, sent, back_send_sem).wait()
    came = back.at[pl.ds(0, n_dev - 1)]
    own_back.wait()
    pltpu.make_async_copy(came, came, back_recv_sem).wait()


def combine_kernel(
    cap, ids, slots, gate, back, in_vmem, out_vmem, token_grad, gate_grad, in_grad, out_grad, wide, rows_back, sem
):
    copies = [
        pltpu.make_async_copy(in_vmem, in_grad, sem.at[0]),
        pltpu.make_async_copy(out_vmem, out_grad, sem.at[1]),
    ]
    for copy in copies:
        copy.start()
    n_dev = back.shape[0]
    tokens, width = token_grad.shape
    blocks = width // LANES
    wide[...] = back[...].astype(F32).reshape(n_dev * MSG, LANES)
    for c in range(cap):
        for b in range(blocks):
            rows_back[c * n_dev : (c + 1) * n_dev, b * LANES : (b + 1) * LANES] = wide[
                pl.ds(c * blocks + b, n_dev, stride=MSG), :
            ].astype(BF16)
    high = wide[pl.ds(cap * blocks, n_dev, stride=MSG), :].astype(BF16)
    low = wide[pl.ds(cap * blocks + 1, n_dev, stride=MSG), :].astype(BF16)
    target = jnp.where(slots[...] >= 0, slots[...] * n_dev + ids[...], -1)
    column = jnp.broadcast_to(target.astype(F32), (LANES, tokens)).T
    lane = lax.broadcasted_iota(jnp.int32, (tokens, LANES), 1).astype(F32)
    hits = [
        jnp.where(column == lane + (k * LANES), 1.0, 0.0).astype(BF16)
        for k in range(cap * n_dev // LANES)
    ]
    token_grad[...] = jnp.dot(
        jnp.concatenate(hits, axis=1), rows_back[...], preferred_element_type=F32
    ).astype(BF16)
    expert = lax.broadcasted_iota(jnp.int32, (n_dev, tokens), 0) == ids[...]
    expert = expert.astype(BF16)
    products = lax.dot_general(high, expert, TN, preferred_element_type=F32)
    products += lax.dot_general(low, expert, TN, preferred_element_type=F32)
    chosen = lax.broadcasted_iota(jnp.int32, (LANES, tokens), 0) == slots[...]
    picked = jnp.sum(jnp.where(chosen, products, 0.0)[0:8], axis=0, keepdims=True)
    gate_grad[...] = picked / gate[...]
    for copy in copies:
        copy.wait()


def shards(output_grad, gate_prob, expert_ids, slots, expert_inputs, w_in, w_out):
    n_node = lax.axis_size("node")
    n_local = lax.axis_size("local")
    n_dev = n_node * n_local
    rows = expert_inputs.shape[1]
    cap = rows // n_dev
    tokens, width = output_grad.shape
    ff = w_in.shape[2]
    ids = expert_ids.reshape(1, tokens)
    place = slots.reshape(1, tokens)
    gate = gate_prob.reshape(1, tokens)
    anywhere = pl.BlockSpec(memory_space=pl.ANY)
    vmem = pl.BlockSpec(memory_space=pltpu.VMEM)
    part = n_dev // 2
    dma = pltpu.SemaphoreType.DMA
    back, in_vmem, out_vmem = pl.pallas_call(
        functools.partial(exchange_kernel, n_node, n_local, cap),
        out_shape=[
            pltpu.VMEM((n_dev, MSG, LANES), BF16),
            pltpu.VMEM((width, ff), BF16),
            pltpu.VMEM((ff, width), BF16),
        ],
        in_specs=[vmem] * 3 + [anywhere] * 4,
        out_specs=[vmem] * 3,
        scratch_shapes=[
            pltpu.VMEM((tokens, width), BF16),
            pltpu.VMEM((rows, width), BF16),
            pltpu.VMEM((width, ff), BF16),
            pltpu.VMEM((ff, width), BF16),
            pltpu.VMEM((rows, width), BF16),
            pltpu.VMEM((width, rows), BF16),
            pltpu.VMEM((rows, ff), BF16),
            pltpu.VMEM((rows, ff), F32),
            pltpu.VMEM((rows, ff), BF16),
            pltpu.VMEM((rows, width), BF16),
            pltpu.VMEM((n_dev * MSG, LANES), F32),
            pltpu.VMEM((n_dev, MSG, LANES), BF16),
            pltpu.VMEM((2, part, MSG, LANES), BF16),
            pltpu.VMEM((2, part, MSG, LANES), BF16),
            dma((4,)),
            dma,
            dma,
            dma((2,)),
            dma,
            dma,
        ],
        compiler_params=pltpu.CompilerParams(
            collective_id=0, has_side_effects=True, vmem_limit_bytes=VMEM_LIMIT
        ),
        name="exchange",
    )(ids, place, gate, output_grad, expert_inputs[0], w_in[0], w_out[0])

    token_grad, gate_grad, in_grad, out_grad = pl.pallas_call(
        functools.partial(combine_kernel, cap),
        out_shape=[
            jax.ShapeDtypeStruct((tokens, width), BF16),
            jax.ShapeDtypeStruct((1, tokens), F32),
            jax.ShapeDtypeStruct((width, ff), BF16),
            jax.ShapeDtypeStruct((ff, width), BF16),
        ],
        in_specs=[vmem] * 6,
        out_specs=[vmem, vmem, anywhere, anywhere],
        scratch_shapes=[
            pltpu.VMEM((n_dev * MSG, LANES), F32),
            pltpu.VMEM((rows, width), BF16),
            dma((2,)),
        ],
        compiler_params=pltpu.CompilerParams(vmem_limit_bytes=16 * 1024 * 1024),
        name="combine",
    )(ids, place, gate, back, in_vmem, out_vmem)
    return (token_grad, gate_grad.reshape(tokens), in_grad[None], out_grad[None])


def solution(mesh):
    placed = (
        P(("node", "local"), None),
        P(("node", "local")),
        P(("node", "local")),
        P(("node", "local")),
        P(("node", "local"), None, None),
        P(("node", "local"), None, None),
        P(("node", "local"), None, None),
    )
    return jax.shard_map(
        shards,
        mesh=mesh,
        in_specs=placed,
        out_specs=(
            P(("node", "local"), None),
            P(("node", "local")),
            P(("node", "local"), None, None),
            P(("node", "local"), None, None),
        ),
        check_vma=False,
    )
```

```python
import functools
import math

import jax
import jax.numpy as jnp
from jax import lax
from jax.experimental import pallas as pl
from jax.experimental.pallas import tpu as pltpu
from jax.sharding import PartitionSpec as P

MESH = pl.DeviceIdType.MESH
F32 = jnp.float32
BF16 = jnp.bfloat16
LANES = 128
MSG = 32
NT = (((1,), (1,)), ((), ()))
TN = (((0,), (0,)), ((), ()))
VMEM_LIMIT = 44 * 1024 * 1024
FWD_TILE = 1536
BWD_TILE = 3072
GRAD_TILE = 3072


def signal(sem, device):
    pl.semaphore_signal(sem, inc=1, device_id=device, device_id_type=MESH)


def exchange_kernel(
    n_node, n_local, cap, ids_hbm, slots_hbm, gate_hbm, og_hbm, x_hbm, win_hbm, wout_hbm,
    back, in_grad, out_grad,
    ids, slots, gate, og, x, win, wout, xp, x_t, hid, slope, pg, routed, wide, msg, recv, ret,
    in_sem, own_sem, send_sem, recv_sem, back_send_sem, back_recv_sem,
):
    node, local = lax.axis_index("node"), lax.axis_index("local")
    n_dev = n_node * n_local
    me = node * n_local + local
    core, pair = node % 2, node // 2
    n_pair = n_node // 2
    part = n_pair * n_local
    place = pair * n_local + local
    rows, width = xp.shape
    half = part * cap
    blocks = width // LANES
    ff = hid.shape[1]

    loads = [
        pltpu.make_async_copy(src, dst, in_sem.at[k])
        for k, (src, dst) in enumerate(
            (
                (og_hbm, og),
                (x_hbm, x),
                (win_hbm, win),
                (wout_hbm, wout),
                (ids_hbm, ids),
                (slots_hbm, slots),
                (gate_hbm, gate),
            )
        )
    ]
    early = (loads[4], loads[5], loads[6], loads[0])
    for load in early:
        load.start()

    barrier = pltpu.get_barrier_semaphore()

    def greet(k, carry):
        for j in range(n_local):
            signal(barrier, ((node + k) % n_node, j))
        return carry

    for k in range(1, n_node):
        greet(k, 0)
    for j in range(1, n_local):
        signal(barrier, (node, (local + j) % n_local))

    for load in early:
        load.wait()
    for load in loads[1:4]:
        load.start()
    target = jnp.where(slots[...] >= 0, slots[...] * n_dev + ids[...], -1)
    tokens = target.shape[1]
    for c in range(cap):
        hit = lax.broadcasted_iota(jnp.int32, (n_dev, tokens), 0) + c * n_dev == target
        moved = jnp.dot(hit.astype(BF16), og[...], preferred_element_type=F32)
        factor = jnp.sum(jnp.where(hit, gate[...], 0.0), axis=1, keepdims=True)
        moved = moved * factor
        for b in range(blocks):
            wide[pl.ds(c * blocks + b, n_dev, stride=MSG), :] = moved[:, b * LANES : (b + 1) * LANES]
    msg[...] = wide[...].reshape(n_dev, MSG, LANES).astype(BF16)

    pl.semaphore_wait(barrier, n_dev - 1)

    def peer(step, k):
        there = (place + k) % part
        return 2 * (there // n_local) + (core + step) % 2, there % n_local, there

    own = pltpu.make_async_copy(msg.at[me], recv.at[0, place], own_sem)
    own.start()
    def send(step, k):
        to_node, to_local, there = peer(step, k)
        pltpu.make_async_remote_copy(
            src_ref=msg.at[to_node * n_local + to_local],
            dst_ref=recv.at[step, place],
            send_sem=send_sem,
            recv_sem=recv_sem.at[step],
            device_id=(to_node, to_local),
            device_id_type=MESH,
        ).start()

    for k in range(1, part):
        send(0, k)

    loads[1].wait()
    for step in range(2):
        r = lax.broadcasted_iota(jnp.int32, (half, rows), 0)
        c, i = r // part, r % part
        source = (i // n_local) * (2 * n_local) + ((core + step) % 2) * n_local + i % n_local
        hit = lax.broadcasted_iota(jnp.int32, (half, rows), 1) == source * cap + c
        ordered = jnp.dot(hit.astype(BF16), x[...], preferred_element_type=F32).astype(BF16)
        xp[step * half : (step + 1) * half, :] = ordered

    loads[2].wait()
    tile = FWD_TILE
    wide_tile = GRAD_TILE

    def forward(k, carry):
        cols = pl.ds(k * tile if isinstance(k, int) else pl.multiple_of(k * tile, tile), tile)
        pre = jnp.dot(xp[...], win[:, cols], preferred_element_type=F32)
        cdf = 0.5 * (1.0 + lax.erf(pre * (1.0 / math.sqrt(2.0))))
        dens = jnp.exp(-0.5 * pre * pre) * (1.0 / math.sqrt(2.0 * math.pi))
        hidden = (pre * cdf).astype(BF16)
        hid[:, cols] = hidden
        slope[:, cols] = cdf + pre * dens
        return carry

    n_tiles = ff // tile
    for t in range(n_tiles):
        forward(t, 0)
    for k in range(part):
        send(1, k)
    own.wait()
    loads[3].wait()
    tile = BWD_TILE

    own_back = pltpu.make_async_copy(ret.at[0, place], back.at[me], own_sem)
    for step in range(2):
        mine = slice(step * half, (step + 1) * half)
        n_in = part - 1 + step
        got = recv.at[step, pl.ds(0, n_in)]
        pltpu.make_async_copy(got, got, recv_sem.at[step]).wait()
        wide[0 : part * MSG, :] = recv[step].astype(F32).reshape(part * MSG, LANES)
        for c in range(cap):
            for b in range(blocks):
                routed[step * half + c * part : step * half + (c + 1) * part, b * LANES : (b + 1) * LANES] = (
                    wide[pl.ds(c * blocks + b, part, stride=MSG), :].astype(BF16)
                )

        def backward(k, total, mine=mine):
            cols = pl.ds(k * tile if isinstance(k, int) else pl.multiple_of(k * tile, tile), tile)
            up = lax.dot_general(routed[mine, :], wout[cols, :], NT, preferred_element_type=F32)
            pg[mine, cols] = (up * slope[mine, cols]).astype(BF16)
            both = up * hid[mine, cols].astype(F32)
            for b in range(tile // LANES):
                total = total + both[:, b * LANES : (b + 1) * LANES]
            return total

        total = lax.fori_loop(0, ff // tile, backward, jnp.zeros((half, LANES), F32))
        product = jnp.sum(total, axis=1, keepdims=True)
        lane = lax.broadcasted_iota(jnp.int32, (part, LANES), 1)
        spread = jnp.zeros((part, LANES), F32)
        for c in range(cap):
            spread = jnp.where(lane == c, product[c * part : (c + 1) * part], spread)
        high = spread.astype(BF16).astype(F32)
        wide[pl.ds(cap * blocks, part, stride=MSG), :] = high
        wide[pl.ds(cap * blocks + 1, part, stride=MSG), :] = spread - high
        for q in range(width // 256):
            down = lax.dot_general(
                pg[mine, :], win[q * 256 : (q + 1) * 256, :], NT, preferred_element_type=F32
            )
            for c in range(cap):
                for b in range(2):
                    wide[pl.ds(c * blocks + 2 * q + b, part, stride=MSG), :] = down[
                        c * part : (c + 1) * part, b * LANES : (b + 1) * LANES
                    ]
        ret[step] = wide[0 : part * MSG, :].reshape(part, MSG, LANES).astype(BF16)
        if step == 0:
            own_back.start()

        def reply(k, carry, step=step):
            to_node, to_local, there = peer(step, k)
            pltpu.make_async_remote_copy(
                src_ref=ret.at[step, there],
                dst_ref=back.at[me],
                send_sem=back_send_sem,
                recv_sem=back_recv_sem,
                device_id=(to_node, to_local),
                device_id_type=MESH,
            ).start()
            return carry

        for k in range(1 - step, part):
            reply(k, 0)

    def out_tile(k, carry):
        part_rows = pl.ds(pl.multiple_of(k * wide_tile, wide_tile), wide_tile)
        out_grad[part_rows, :] = lax.dot_general(
            hid[:, part_rows], routed[...], TN, preferred_element_type=F32
        ).astype(BF16)
        return carry

    x_t[...] = xp[...].T

    def in_tile(k, carry):
        cols = pl.ds(pl.multiple_of(k * wide_tile, wide_tile), wide_tile)
        in_grad[:, cols] = jnp.dot(x_t[...], pg[:, cols], preferred_element_type=F32).astype(BF16)
        return carry

    lax.fori_loop(0, ff // wide_tile, out_tile, 0)
    lax.fori_loop(0, ff // wide_tile, in_tile, 0)
    sent = msg.at[pl.ds(0, n_dev - 1)]
    pltpu.make_async_copy(sent, sent, send_sem).wait()
    pltpu.make_async_copy(sent, sent, back_send_sem).wait()
    came = back.at[pl.ds(0, n_dev - 1)]
    own_back.wait()
    pltpu.make_async_copy(came, came, back_recv_sem).wait()


def combine_kernel(
    cap, ids, slots, gate, back, in_vmem, out_vmem, token_hbm, gate_grad, in_grad, out_grad, wide, rows_back, token_grad, sem
):
    copies = [
        pltpu.make_async_copy(in_vmem, in_grad, sem.at[0]),
        pltpu.make_async_copy(out_vmem, out_grad, sem.at[1]),
    ]
    for copy in copies:
        copy.start()
    n_dev = back.shape[0]
    tokens, width = token_grad.shape
    blocks = width // LANES
    wide[...] = back[...].astype(F32).reshape(n_dev * MSG, LANES)
    for c in range(cap):
        for b in range(blocks):
            rows_back[c * n_dev : (c + 1) * n_dev, b * LANES : (b + 1) * LANES] = wide[
                pl.ds(c * blocks + b, n_dev, stride=MSG), :
            ].astype(BF16)
    high = wide[pl.ds(cap * blocks, n_dev, stride=MSG), :].astype(BF16)
    low = wide[pl.ds(cap * blocks + 1, n_dev, stride=MSG), :].astype(BF16)
    target = jnp.where(slots[...] >= 0, slots[...] * n_dev + ids[...], -1)
    column = jnp.broadcast_to(target.astype(F32), (LANES, tokens)).T
    lane = lax.broadcasted_iota(jnp.int32, (tokens, LANES), 1).astype(F32)
    hits = [
        jnp.where(column == lane + (k * LANES), 1.0, 0.0).astype(BF16)
        for k in range(cap * n_dev // LANES)
    ]
    token_grad[...] = jnp.dot(
        jnp.concatenate(hits, axis=1), rows_back[...], preferred_element_type=F32
    ).astype(BF16)
    copies.append(pltpu.make_async_copy(token_grad, token_hbm, sem.at[2]))
    copies[2].start()
    expert = lax.broadcasted_iota(jnp.int32, (n_dev, tokens), 0) == ids[...]
    expert = expert.astype(BF16)
    products = lax.dot_general(high, expert, TN, preferred_element_type=F32)
    products += lax.dot_general(low, expert, TN, preferred_element_type=F32)
    chosen = lax.broadcasted_iota(jnp.int32, (LANES, tokens), 0) == slots[...]
    picked = jnp.sum(jnp.where(chosen, products, 0.0)[0:8], axis=0, keepdims=True)
    gate_grad[...] = picked / gate[...]
    for copy in copies:
        copy.wait()


def shards(output_grad, gate_prob, expert_ids, slots, expert_inputs, w_in, w_out):
    n_node = lax.axis_size("node")
    n_local = lax.axis_size("local")
    n_dev = n_node * n_local
    rows = expert_inputs.shape[1]
    cap = rows // n_dev
    tokens, width = output_grad.shape
    ff = w_in.shape[2]
    ids = expert_ids.reshape(1, tokens)
    place = slots.reshape(1, tokens)
    gate = gate_prob.reshape(1, tokens)
    anywhere = pl.BlockSpec(memory_space=pl.ANY)
    vmem = pl.BlockSpec(memory_space=pltpu.VMEM)
    part = n_dev // 2
    dma = pltpu.SemaphoreType.DMA
    back, in_vmem, out_vmem = pl.pallas_call(
        functools.partial(exchange_kernel, n_node, n_local, cap),
        out_shape=[
            pltpu.VMEM((n_dev, MSG, LANES), BF16),
            pltpu.VMEM((width, ff), BF16),
            pltpu.VMEM((ff, width), BF16),
        ],
        in_specs=[anywhere] * 7,
        out_specs=[vmem] * 3,
        scratch_shapes=[
            pltpu.VMEM((1, tokens), jnp.int32),
            pltpu.VMEM((1, tokens), jnp.int32),
            pltpu.VMEM((1, tokens), F32),
            pltpu.VMEM((tokens, width), BF16),
            pltpu.VMEM((rows, width), BF16),
            pltpu.VMEM((width, ff), BF16),
            pltpu.VMEM((ff, width), BF16),
            pltpu.VMEM((rows, width), BF16),
            pltpu.VMEM((width, rows), BF16),
            pltpu.VMEM((rows, ff), BF16),
            pltpu.VMEM((rows, ff), F32),
            pltpu.VMEM((rows, ff), BF16),
            pltpu.VMEM((rows, width), BF16),
            pltpu.VMEM((n_dev * MSG, LANES), F32),
            pltpu.VMEM((n_dev, MSG, LANES), BF16),
            pltpu.VMEM((2, part, MSG, LANES), BF16),
            pltpu.VMEM((2, part, MSG, LANES), BF16),
            dma((7,)),
            dma,
            dma,
            dma((2,)),
            dma,
            dma,
        ],
        compiler_params=pltpu.CompilerParams(
            collective_id=0, has_side_effects=True, vmem_limit_bytes=VMEM_LIMIT
        ),
        name="exchange",
    )(ids, place, gate, output_grad, expert_inputs[0], w_in[0], w_out[0])

    token_grad, gate_grad, in_grad, out_grad = pl.pallas_call(
        functools.partial(combine_kernel, cap),
        out_shape=[
            jax.ShapeDtypeStruct((tokens, width), BF16),
            jax.ShapeDtypeStruct((1, tokens), F32),
            jax.ShapeDtypeStruct((width, ff), BF16),
            jax.ShapeDtypeStruct((ff, width), BF16),
        ],
        in_specs=[vmem] * 6,
        out_specs=[anywhere, vmem, anywhere, anywhere],
        scratch_shapes=[
            pltpu.VMEM((n_dev * MSG, LANES), F32),
            pltpu.VMEM((rows, width), BF16),
            pltpu.VMEM((tokens, width), BF16),
            dma((3,)),
        ],
        compiler_params=pltpu.CompilerParams(vmem_limit_bytes=16 * 1024 * 1024),
        name="combine",
    )(ids, place, gate, back, in_vmem, out_vmem)
    return (token_grad, gate_grad.reshape(tokens), in_grad[None], out_grad[None])


def solution(mesh):
    placed = (
        P(("node", "local"), None),
        P(("node", "local")),
        P(("node", "local")),
        P(("node", "local")),
        P(("node", "local"), None, None),
        P(("node", "local"), None, None),
        P(("node", "local"), None, None),
    )
    return jax.shard_map(
        shards,
        mesh=mesh,
        in_specs=placed,
        out_specs=(
            P(("node", "local"), None),
            P(("node", "local")),
            P(("node", "local"), None, None),
            P(("node", "local"), None, None),
        ),
        check_vma=False,
    )
```

```python
import functools
import math

import jax
import jax.numpy as jnp
from jax import lax
from jax.experimental import pallas as pl
from jax.experimental.pallas import tpu as pltpu
from jax.sharding import PartitionSpec as P

MESH = pl.DeviceIdType.MESH
F32 = jnp.float32
BF16 = jnp.bfloat16
LANES = 128
MSG = 32
NT = (((1,), (1,)), ((), ()))
TN = (((0,), (0,)), ((), ()))
VMEM_LIMIT = 44 * 1024 * 1024
FWD_TILE = 1536
BWD_TILE = 3072
GRAD_TILE = 3072


def signal(sem, device):
    pl.semaphore_signal(sem, inc=1, device_id=device, device_id_type=MESH)


def exchange_kernel(
    n_node, n_local, cap, ids_hbm, slots_hbm, gate_hbm, og_hbm, x_hbm, win_hbm, wout_hbm,
    back, in_grad, out_grad,
    ids, slots, gate, og, x, win, wout, xp, x_t, hid, slope, pg, routed, wide, msg, recv, ret,
    in_sem, own_sem, send_sem, recv_sem, back_send_sem, back_recv_sem,
):
    node, local = lax.axis_index("node"), lax.axis_index("local")
    n_dev = n_node * n_local
    me = node * n_local + local
    core, pair = node % 2, node // 2
    n_pair = n_node // 2
    part = n_pair * n_local
    place = pair * n_local + local
    rows, width = xp.shape
    half = part * cap
    blocks = width // LANES
    ff = hid.shape[1]

    loads = [
        pltpu.make_async_copy(src, dst, in_sem.at[k])
        for k, (src, dst) in enumerate(
            (
                (og_hbm, og),
                (x_hbm, x),
                (win_hbm, win),
                (wout_hbm, wout),
                (ids_hbm, ids),
                (slots_hbm, slots),
                (gate_hbm, gate),
            )
        )
    ]
    early = (loads[4], loads[5], loads[6], loads[0])
    for load in early:
        load.start()

    barrier = pltpu.get_barrier_semaphore()

    def greet(k, carry):
        for j in range(n_local):
            signal(barrier, ((node + k) % n_node, j))
        return carry

    for k in range(1, n_node):
        greet(k, 0)
    for j in range(1, n_local):
        signal(barrier, (node, (local + j) % n_local))

    for load in early:
        load.wait()
    for load in loads[1:4]:
        load.start()
    target = jnp.where(slots[...] >= 0, slots[...] * n_dev + ids[...], -1)
    tokens = target.shape[1]
    for c in range(cap):
        hit = lax.broadcasted_iota(jnp.int32, (n_dev, tokens), 0) + c * n_dev == target
        moved = jnp.dot(hit.astype(BF16), og[...], preferred_element_type=F32)
        factor = jnp.sum(jnp.where(hit, gate[...], 0.0), axis=1, keepdims=True)
        moved = moved * factor
        for b in range(blocks):
            wide[pl.ds(c * blocks + b, n_dev, stride=MSG), :] = moved[:, b * LANES : (b + 1) * LANES]
    msg[...] = wide[...].reshape(n_dev, MSG, LANES).astype(BF16)

    pl.semaphore_wait(barrier, n_dev - 1)

    def peer(step, k):
        there = (place + k) % part
        return 2 * (there // n_local) + (core + step) % 2, there % n_local, there

    own = pltpu.make_async_copy(msg.at[me], recv.at[0, place], own_sem)
    own.start()
    def send(step, k):
        to_node, to_local, there = peer(step, k)
        pltpu.make_async_remote_copy(
            src_ref=msg.at[to_node * n_local + to_local],
            dst_ref=recv.at[step, place],
            send_sem=send_sem,
            recv_sem=recv_sem.at[step],
            device_id=(to_node, to_local),
            device_id_type=MESH,
        ).start()

    for k in range(1, part):
        send(0, k)

    loads[1].wait()
    for step in range(2):
        r = lax.broadcasted_iota(jnp.int32, (half, rows), 0)
        c, i = r // part, r % part
        source = (i // n_local) * (2 * n_local) + ((core + step) % 2) * n_local + i % n_local
        hit = lax.broadcasted_iota(jnp.int32, (half, rows), 1) == source * cap + c
        ordered = jnp.dot(hit.astype(BF16), x[...], preferred_element_type=F32).astype(BF16)
        xp[step * half : (step + 1) * half, :] = ordered

    loads[2].wait()
    tile = FWD_TILE
    wide_tile = GRAD_TILE

    def forward(k, carry):
        cols = pl.ds(k * tile if isinstance(k, int) else pl.multiple_of(k * tile, tile), tile)
        pre = jnp.dot(xp[...], win[:, cols], preferred_element_type=F32)
        cdf = 0.5 * (1.0 + lax.erf(pre * (1.0 / math.sqrt(2.0))))
        dens = jnp.exp(-0.5 * pre * pre) * (1.0 / math.sqrt(2.0 * math.pi))
        hidden = (pre * cdf).astype(BF16)
        hid[:, cols] = hidden
        slope[:, cols] = cdf + pre * dens
        return carry

    n_tiles = ff // tile
    for t in range(n_tiles):
        forward(t, 0)
    for k in range(part):
        send(1, k)
    own.wait()
    loads[3].wait()
    tile = BWD_TILE

    own_back = pltpu.make_async_copy(ret.at[0, place], back.at[me], own_sem)
    for step in range(2):
        mine = slice(step * half, (step + 1) * half)
        n_in = part - 1 + step
        got = recv.at[step, pl.ds(0, n_in)]
        pltpu.make_async_copy(got, got, recv_sem.at[step]).wait()
        wide[0 : part * MSG, :] = recv[step].astype(F32).reshape(part * MSG, LANES)
        for c in range(cap):
            for b in range(blocks):
                routed[step * half + c * part : step * half + (c + 1) * part, b * LANES : (b + 1) * LANES] = (
                    wide[pl.ds(c * blocks + b, part, stride=MSG), :].astype(BF16)
                )

        def backward(k, total, mine=mine):
            cols = pl.ds(k * tile if isinstance(k, int) else pl.multiple_of(k * tile, tile), tile)
            up = lax.dot_general(routed[mine, :], wout[cols, :], NT, preferred_element_type=F32)
            pg[mine, cols] = (up * slope[mine, cols]).astype(BF16)
            both = up * hid[mine, cols].astype(F32)
            for b in range(tile // LANES):
                total = total + both[:, b * LANES : (b + 1) * LANES]
            return total

        total = lax.fori_loop(0, ff // tile, backward, jnp.zeros((half, LANES), F32))
        product = jnp.sum(total, axis=1, keepdims=True)
        lane = lax.broadcasted_iota(jnp.int32, (part, LANES), 1)
        spread = jnp.zeros((part, LANES), F32)
        for c in range(cap):
            spread = jnp.where(lane == c, product[c * part : (c + 1) * part], spread)
        high = spread.astype(BF16).astype(F32)
        wide[pl.ds(cap * blocks, part, stride=MSG), :] = high
        wide[pl.ds(cap * blocks + 1, part, stride=MSG), :] = spread - high
        for q in range(width // 256):
            down = lax.dot_general(
                pg[mine, :], win[q * 256 : (q + 1) * 256, :], NT, preferred_element_type=F32
            )
            for c in range(cap):
                for b in range(2):
                    wide[pl.ds(c * blocks + 2 * q + b, part, stride=MSG), :] = down[
                        c * part : (c + 1) * part, b * LANES : (b + 1) * LANES
                    ]
        ret[step] = wide[0 : part * MSG, :].reshape(part, MSG, LANES).astype(BF16)
        if step == 0:
            own_back.start()

        def reply(k, carry, step=step):
            to_node, to_local, there = peer(step, k)
            pltpu.make_async_remote_copy(
                src_ref=ret.at[step, there],
                dst_ref=back.at[me],
                send_sem=back_send_sem,
                recv_sem=back_recv_sem,
                device_id=(to_node, to_local),
                device_id_type=MESH,
            ).start()
            return carry

        for k in range(1 - step, part):
            reply(k, 0)

    def out_tile(k, carry):
        part_rows = pl.ds(pl.multiple_of(k * wide_tile, wide_tile), wide_tile)
        out_grad[part_rows, :] = lax.dot_general(
            hid[:, part_rows], routed[...], TN, preferred_element_type=F32
        ).astype(BF16)
        return carry

    x_t[...] = xp[...].T

    def in_tile(k, carry):
        cols = pl.ds(pl.multiple_of(k * wide_tile, wide_tile), wide_tile)
        in_grad[:, cols] = jnp.dot(x_t[...], pg[:, cols], preferred_element_type=F32).astype(BF16)
        return carry

    lax.fori_loop(0, ff // wide_tile, out_tile, 0)
    lax.fori_loop(0, ff // wide_tile, in_tile, 0)
    sent = msg.at[pl.ds(0, n_dev - 1)]
    pltpu.make_async_copy(sent, sent, send_sem).wait()
    pltpu.make_async_copy(sent, sent, back_send_sem).wait()
    came = back.at[pl.ds(0, n_dev - 1)]
    own_back.wait()
    pltpu.make_async_copy(came, came, back_recv_sem).wait()


def combine_kernel(
    cap, ids, slots, gate, back, in_vmem, out_vmem, token_hbm, gate_hbm, in_grad, out_grad, wide, rows_back, token_grad, gate_grad, sem
):
    copies = [
        pltpu.make_async_copy(in_vmem, in_grad, sem.at[0]),
        pltpu.make_async_copy(out_vmem, out_grad, sem.at[1]),
    ]
    for copy in copies:
        copy.start()
    n_dev = back.shape[0]
    tokens, width = token_grad.shape
    blocks = width // LANES
    wide[...] = back[...].astype(F32).reshape(n_dev * MSG, LANES)
    for c in range(cap):
        for b in range(blocks):
            rows_back[c * n_dev : (c + 1) * n_dev, b * LANES : (b + 1) * LANES] = wide[
                pl.ds(c * blocks + b, n_dev, stride=MSG), :
            ].astype(BF16)
    high = wide[pl.ds(cap * blocks, n_dev, stride=MSG), :].astype(BF16)
    low = wide[pl.ds(cap * blocks + 1, n_dev, stride=MSG), :].astype(BF16)
    target = jnp.where(slots[...] >= 0, slots[...] * n_dev + ids[...], -1)
    column = jnp.broadcast_to(target.astype(F32), (LANES, tokens)).T
    lane = lax.broadcasted_iota(jnp.int32, (tokens, LANES), 1).astype(F32)
    hits = [
        jnp.where(column == lane + (k * LANES), 1.0, 0.0).astype(BF16)
        for k in range(cap * n_dev // LANES)
    ]
    token_grad[...] = jnp.dot(
        jnp.concatenate(hits, axis=1), rows_back[...], preferred_element_type=F32
    ).astype(BF16)
    copies.append(pltpu.make_async_copy(token_grad, token_hbm, sem.at[2]))
    copies[2].start()
    expert = lax.broadcasted_iota(jnp.int32, (n_dev, tokens), 0) == ids[...]
    expert = expert.astype(BF16)
    products = lax.dot_general(high, expert, TN, preferred_element_type=F32)
    products += lax.dot_general(low, expert, TN, preferred_element_type=F32)
    chosen = lax.broadcasted_iota(jnp.int32, (LANES, tokens), 0) == slots[...]
    picked = jnp.sum(jnp.where(chosen, products, 0.0)[0:8], axis=0, keepdims=True)
    gate_grad[...] = picked / gate[...]
    copies.append(pltpu.make_async_copy(gate_grad, gate_hbm, sem.at[3]))
    copies[3].start()
    for copy in copies:
        copy.wait()


def shards(output_grad, gate_prob, expert_ids, slots, expert_inputs, w_in, w_out):
    n_node = lax.axis_size("node")
    n_local = lax.axis_size("local")
    n_dev = n_node * n_local
    rows = expert_inputs.shape[1]
    cap = rows // n_dev
    tokens, width = output_grad.shape
    ff = w_in.shape[2]
    ids = expert_ids.reshape(1, tokens)
    place = slots.reshape(1, tokens)
    gate = gate_prob.reshape(1, tokens)
    anywhere = pl.BlockSpec(memory_space=pl.ANY)
    vmem = pl.BlockSpec(memory_space=pltpu.VMEM)
    part = n_dev // 2
    dma = pltpu.SemaphoreType.DMA
    back, in_vmem, out_vmem = pl.pallas_call(
        functools.partial(exchange_kernel, n_node, n_local, cap),
        out_shape=[
            pltpu.VMEM((n_dev, MSG, LANES), BF16),
            pltpu.VMEM((width, ff), BF16),
            pltpu.VMEM((ff, width), BF16),
        ],
        in_specs=[anywhere] * 7,
        out_specs=[vmem] * 3,
        scratch_shapes=[
            pltpu.VMEM((1, tokens), jnp.int32),
            pltpu.VMEM((1, tokens), jnp.int32),
            pltpu.VMEM((1, tokens), F32),
            pltpu.VMEM((tokens, width), BF16),
            pltpu.VMEM((rows, width), BF16),
            pltpu.VMEM((width, ff), BF16),
            pltpu.VMEM((ff, width), BF16),
            pltpu.VMEM((rows, width), BF16),
            pltpu.VMEM((width, rows), BF16),
            pltpu.VMEM((rows, ff), BF16),
            pltpu.VMEM((rows, ff), F32),
            pltpu.VMEM((rows, ff), BF16),
            pltpu.VMEM((rows, width), BF16),
            pltpu.VMEM((n_dev * MSG, LANES), F32),
            pltpu.VMEM((n_dev, MSG, LANES), BF16),
            pltpu.VMEM((2, part, MSG, LANES), BF16),
            pltpu.VMEM((2, part, MSG, LANES), BF16),
            dma((7,)),
            dma,
            dma,
            dma((2,)),
            dma,
            dma,
        ],
        compiler_params=pltpu.CompilerParams(
            collective_id=0, has_side_effects=True, vmem_limit_bytes=VMEM_LIMIT
        ),
        name="exchange",
    )(ids, place, gate, output_grad, expert_inputs[0], w_in[0], w_out[0])

    token_grad, gate_grad, in_grad, out_grad = pl.pallas_call(
        functools.partial(combine_kernel, cap),
        out_shape=[
            jax.ShapeDtypeStruct((tokens, width), BF16),
            jax.ShapeDtypeStruct((1, tokens), F32),
            jax.ShapeDtypeStruct((width, ff), BF16),
            jax.ShapeDtypeStruct((ff, width), BF16),
        ],
        in_specs=[vmem] * 6,
        out_specs=[anywhere] * 4,
        scratch_shapes=[
            pltpu.VMEM((n_dev * MSG, LANES), F32),
            pltpu.VMEM((rows, width), BF16),
            pltpu.VMEM((tokens, width), BF16),
            pltpu.VMEM((1, tokens), F32),
            dma((4,)),
        ],
        compiler_params=pltpu.CompilerParams(vmem_limit_bytes=16 * 1024 * 1024),
        name="combine",
    )(ids, place, gate, back, in_vmem, out_vmem)
    return (token_grad, gate_grad.reshape(tokens), in_grad[None], out_grad[None])


def solution(mesh):
    placed = (
        P(("node", "local"), None),
        P(("node", "local")),
        P(("node", "local")),
        P(("node", "local")),
        P(("node", "local"), None, None),
        P(("node", "local"), None, None),
        P(("node", "local"), None, None),
    )
    return jax.shard_map(
        shards,
        mesh=mesh,
        in_specs=placed,
        out_specs=(
            P(("node", "local"), None),
            P(("node", "local")),
            P(("node", "local"), None, None),
            P(("node", "local"), None, None),
        ),
        check_vma=False,
    )
```
